32 devices in a mesh: row: 8 (over z, x), col: 4 (over y, core).
Axes of the slice: x: 2, y: 2, z: 4, core: 2. Of those that a mesh axis runs over, the one named last changes fastest.
Arguments:
- tokens: bfloat16 [4, 320, 768], P(None, 'row'), may hold values from -6 to 6
- single_cond: bfloat16 [320, 384], P('row'), may hold values from -6 to 6
- pair_cond: float32 [320, 320, 128], P('row', 'col'), may hold values from -8 to 8
- ada_gain: float32 [2, 384], replicated, may hold values from 0.1 to 1.9
- ada_scale_w: bfloat16 [2, 384, 768], P(None, None, 'col'), may hold values from -0.3125 to 0.3125
- ada_scale_b: float32 [2, 768], P(None, 'col'), may hold values from -4 to 4
- adaptive_shift_weight: bfloat16 [2, 384, 768], P(None, None, 'col'), may hold values from -0.3125 to 0.3125
- pair_gain: float32 [128], replicated, may hold values from 0.1 to 1.9
- pair_proj: float32 [128, 16], replicated, may hold values from -8 to 8
- qkvg_weight: bfloat16 [4, 768, 768], P(None, None, 'col'), may hold values from -0.21875 to 0.21875
- query_bias: float32 [768], P('col'), may hold values from -4 to 4
- output_weight: bfloat16 [768, 768], P('col'), may hold values from -0.21875 to 0.21875
- out_gate_w: bfloat16 [2, 384, 768], P(None, None, 'col'), may hold values from -0.3125 to 0.3125
- out_gate_b: float32 [2, 768], P(None, 'col'), may hold values from -4 to 4
- transition_input_weight: bfloat16 [2, 768, 1536], P(None, None, 'col'), may hold values from -0.21875 to 0.21875
- trans_out: bfloat16 [1536, 768], P('col'), may hold values from -0.15625 to 0.15625
Outputs:
- mixed: bfloat16 [4, 320, 768], P(None, 'row', 'col')
The draws below stay inside these ranges and needn't reach their ends.
All inputs are finite; a program needn't handle non-finite values.
Results may differ from the reference program's by a relative error of at most 0.0052.
Values may be sent and summed in bfloat16 or wider, within the bound.
A program may use at most 64 MiB of HBM per device.

```python
import math
import jax
import jax.numpy as jnp
from jax import lax

D = 768
H = 16
CS = 384
CZ = 128
FF = 1536
S = 4
TOKR = 40
DH = 48
N = 320
N_ROW = 8


def draw_tokens(key, part):
    key = jax.random.fold_in(key, 3)
    ramp = 0.5 + jnp.arange(D, dtype=jnp.float32) / (D - 1)
    values = jnp.clip(jax.random.normal(key, (S, N, D), jnp.float32), -4.0, 4.0) * ramp
    return values.astype(jnp.bfloat16)


def draw_pair_cond(key, part):
    key = jax.random.fold_in(key, 5)
    channel_scale = 0.3 * 10.0 ** (jnp.arange(CZ, dtype=jnp.float32) / (CZ - 1))
    values = jnp.clip(jax.random.normal(key, (N, N, CZ), jnp.float32), -2.5, 2.5) * channel_scale
    return values


def draw_pair_proj(key, part):
    key = jax.random.fold_in(key, 7)
    values = jnp.clip(jax.random.normal(key, (CZ, H), jnp.float32), -4.0, 4.0) / math.sqrt(CZ)
    return values


def block_levels(key, dims, cuts, low, largest):
    factor_of = 1.0
    for dim, parts in cuts:
        steps = jax.random.uniform(jax.random.fold_in(jax.random.fold_in(key, 6), dim), (parts,), jnp.float32, low / len(cuts), largest / len(cuts))
        factor_of = factor_of * jnp.repeat(jnp.exp(steps), dims[dim] // parts).reshape((-1,) + (1,) * (len(dims) - 1 - dim))
    return factor_of


def gaussian(own_key, shape, scale, limit, cuts=(), kind=jnp.bfloat16):
    factor_of = block_levels(own_key, shape, cuts, -0.22, 0.18) if cuts else 1.0
    result = jax.random.normal(own_key, shape, jnp.float32) * scale * factor_of
    return jnp.minimum(jnp.maximum(result, -limit), limit).astype(kind)


def setup_inputs(seed: int = 0) -> dict:
    key_list = jax.random.split(jax.random.key(seed), 17)
    return {
        "tokens": draw_tokens(jax.random.fold_in(key_list[16], 71), 0),
        "single_cond": gaussian(key_list[1], (N, CS), 1.0, 6.0, ((0, 8),)),
        "pair_cond": draw_pair_cond(jax.random.fold_in(key_list[16], 71), 0),
        "ada_gain": jnp.clip(1.0 + 0.18 * jax.random.normal(key_list[3], (2, CS), jnp.float32), 0.1, 1.9),
        "ada_scale_w": gaussian(key_list[4], (2, CS, D), CS ** -0.5, 0.3125, ((2, 4),)),
        "ada_scale_b": gaussian(key_list[5], (2, D), 1.0, 4.0, ((1, 4),), jnp.float32),
        "adaptive_shift_weight": gaussian(key_list[6], (2, CS, D), CS ** -0.5, 0.3125, ((2, 4),)),
        "pair_gain": jnp.clip(1.0 + 0.18 * jax.random.normal(key_list[7], (CZ,), jnp.float32), 0.1, 1.9),
        "pair_proj": draw_pair_proj(jax.random.fold_in(key_list[16], 71), 0),
        "qkvg_weight": gaussian(key_list[9], (4, D, D), D ** -0.5, 0.21875, ((2, 4),)),
        "query_bias": gaussian(key_list[10], (D,), 1.0, 4.0, ((0, 4),), jnp.float32),
        "output_weight": gaussian(key_list[11], (D, D), D ** -0.5, 0.21875, ((0, 4),)),
        "out_gate_w": gaussian(key_list[12], (2, CS, D), CS ** -0.5, 0.3125, ((2, 4),)),
        "out_gate_b": gaussian(key_list[13], (2, D), 1.0, 4.0, ((1, 4),), jnp.float32),
        "transition_input_weight": gaussian(key_list[14], (2, D, FF), D ** -0.5, 0.21875, ((2, 4),)),
        "trans_out": gaussian(key_list[15], (FF, D), FF ** -0.5, 0.15625, ((0, 4),)),
    }


epsilon = 1e-05

def layer_norm(values):
    center = values - lax.optimization_barrier(jnp.mean(values, axis=-1, keepdims=True))
    spread = lax.optimization_barrier(jnp.mean(center * center, axis=-1, keepdims=True))
    return center * lax.rsqrt(spread + epsilon)

def reference(tokens, single_cond, pair_cond, ada_gain, ada_scale_w, ada_scale_b, adaptive_shift_weight, pair_gain, pair_proj, qkvg_weight, query_bias, output_weight, out_gate_w, out_gate_b, transition_input_weight, trans_out):
    highest_precision = lax.Precision.HIGHEST
    cond = (layer_norm(single_cond.astype(jnp.float32))[None] * ada_gain[:, None, :]).astype(jnp.bfloat16)

    def adaptive(stream, index):
        scale = jax.nn.sigmoid(jnp.dot(cond[index], ada_scale_w[index], preferred_element_type=jnp.float32) + ada_scale_b[index])
        shift = jnp.dot(cond[index], adaptive_shift_weight[index], preferred_element_type=jnp.float32)
        return (scale * layer_norm(stream) + shift).astype(jnp.bfloat16)

    def out_gate(index):
        return jax.nn.sigmoid(jnp.dot(cond[index], out_gate_w[index], preferred_element_type=jnp.float32) + out_gate_b[index])
    norm_in = adaptive(tokens.astype(jnp.float32), 0)
    project = jnp.einsum('snd,edf->esnf', norm_in.astype(jnp.float32), qkvg_weight.astype(jnp.float32), precision=highest_precision)
    query = (project[0] + query_bias).astype(jnp.bfloat16).astype(jnp.float32).reshape(S, N, H, DH)
    key_heads = project[1].astype(jnp.bfloat16).astype(jnp.float32).reshape(S, N, H, DH)
    value_heads = project[2].astype(jnp.bfloat16).astype(jnp.float32).reshape(S, N, H, DH)
    gates = jax.nn.sigmoid(project[3])

    def block(index):
        start = (index * TOKR).astype(jnp.int32)
        query_block = lax.dynamic_slice_in_dim(query, start, TOKR, 1)
        pair_block = lax.dynamic_slice_in_dim(pair_cond, start, TOKR, 0)
        bias = jnp.einsum('ijc,ch->hij', layer_norm(pair_block) * pair_gain, pair_proj, precision=highest_precision)
        scores = jnp.einsum('sqhd,skhd->shqk', query_block, key_heads, precision=highest_precision) / math.sqrt(DH) + bias[None]
        attention_weights = jax.nn.softmax(scores, axis=-1)
        return jnp.einsum('shqk,skhd->sqhd', attention_weights, value_heads, precision=highest_precision)
    blocks = lax.map(block, jnp.arange(N_ROW, dtype=jnp.int32))
    heads_out = jnp.moveaxis(blocks, 0, 1).reshape(S, N, D)
    attention_result = (gates * heads_out).astype(jnp.bfloat16)
    projected_output = jnp.einsum('rvz,zt->rvt', attention_result.astype(jnp.float32), output_weight.astype(jnp.float32), precision=highest_precision)
    resid = tokens.astype(jnp.float32) + out_gate(0) * projected_output
    middle_norm = adaptive(resid, 1)
    inner = jnp.einsum('snd,edf->esnf', middle_norm.astype(jnp.float32), transition_input_weight.astype(jnp.float32), precision=highest_precision)
    hidden = (jax.nn.silu(inner[0]) * inner[1]).astype(jnp.bfloat16)
    outward = jnp.einsum('snf,fd->snd', hidden.astype(jnp.float32), trans_out.astype(jnp.float32), precision=highest_precision)
    return (resid + out_gate(1) * outward).astype(jnp.bfloat16)
```

```python
import functools
import math

import jax
import jax.numpy as jnp
from jax import lax
from jax.experimental import pallas as pl
from jax.experimental.pallas import tpu as pltpu
from jax.sharding import PartitionSpec as P

H = 16
epsilon = 1e-05
F32 = jnp.float32
BF16 = jnp.bfloat16


def layer_norm(values):
    center = values - jnp.mean(values, axis=-1, keepdims=True)
    spread = jnp.mean(center * center, axis=-1, keepdims=True)
    return center * lax.rsqrt(spread + epsilon)


def dot(a, b):
    return jnp.dot(a, b, preferred_element_type=F32)


def dot_t(a, b):
    return lax.dot_general(a, b, (((1,), (1,)), ((), ())), preferred_element_type=F32)


class Exchange:
    def __init__(self, axis, n, source, buffer, send, recv):
        self.axis, self.n, self.source, self.buffer = axis, n, source, buffer
        self.send, self.recv = send, recv
        self.me = lax.axis_index(axis)

    def copy(self, d):
        target = lax.rem(self.me + d, self.n)
        return pltpu.make_async_remote_copy(
            src_ref=self.source(target),
            dst_ref=self.buffer.at[self.me],
            send_sem=self.send.at[d],
            recv_sem=self.recv.at[self.me],
            device_id={self.axis: target},
            device_id_type=pl.DeviceIdType.MESH,
        )

    def start(self):
        for d in range(1, self.n):
            self.copy(d).start()

    def arrive(self):
        for d in range(1, self.n):
            origin = lax.rem(self.me + d, self.n)
            pltpu.make_async_remote_copy(
                src_ref=self.buffer.at[origin],
                dst_ref=self.buffer.at[origin],
                send_sem=self.send.at[d],
                recv_sem=self.recv.at[origin],
                device_id={self.axis: origin},
                device_id_type=pl.DeviceIdType.MESH,
            ).wait_recv()

    def drain(self):
        for d in range(1, self.n):
            self.copy(d).wait_send()


class PairGather:
    def __init__(self, axis, n, buffer, send, handed, recv):
        self.axis, self.n, self.buffer = axis, n, buffer
        self.send, self.handed, self.recv = send, handed, recv
        self.me = lax.axis_index(axis)
        self.partner = self.me + 1 - 2 * lax.rem(self.me, 2)

    def copy(self, block, target, sem):
        return pltpu.make_async_remote_copy(
            src_ref=self.buffer.at[block],
            dst_ref=self.buffer.at[block],
            send_sem=sem,
            recv_sem=self.recv.at[block],
            device_id={self.axis: target},
            device_id_type=pl.DeviceIdType.MESH,
        )

    def mate(self, d):
        return lax.rem(self.me + 2 * d, self.n)

    def start(self):
        for d in range(1, self.n // 2):
            self.copy(self.me, self.mate(d), self.send.at[d]).start()
        self.copy(self.me, self.partner, self.send.at[0]).start()

    def hand_on(self):
        for d in range(1, self.n // 2):
            block = self.mate(d)
            self.copy(block, self.partner, self.handed.at[d]).wait_recv()
            self.copy(block, self.partner, self.handed.at[d]).start()

    def arrive(self):
        for d in range(self.n // 2):
            block = lax.rem(self.partner + 2 * d, self.n)
            self.copy(block, self.partner, self.send.at[0]).wait_recv()

    def drain(self):
        for d in range(1, self.n // 2):
            self.copy(self.me, self.mate(d), self.send.at[d]).wait_send()
            self.copy(self.mate(d), self.partner, self.handed.at[d]).wait_send()
        self.copy(self.me, self.partner, self.send.at[0]).wait_send()


def kernel(
    n_row,
    n_col,
    tokens_ref,
    single_ref,
    ada_gain_ref,
    scale_b_ref,
    query_b_ref,
    gate_b_ref,
    pair_gain_ref,
    pair_proj_ref,
    scale_w_hbm,
    shift_w_hbm,
    pair_hbm,
    qkvg_hbm,
    gate_w_hbm,
    out_w_hbm,
    trans_in_hbm,
    trans_out_hbm,
    out_ref,
    scale_w,
    shift_w,
    pair,
    qkvg,
    gate_w,
    trans_in,
    trans_out,
    out_w,
    mods0,
    mods1,
    bias_tx,
    bias_rx,
    keys,
    values,
    attended,
    terms32,
    terms_tx,
    terms_rx,
    resid_parts,
    load_sem,
    mods0_send,
    mods0_recv,
    mods1_send,
    mods1_recv,
    bias_send,
    bias_recv,
    att_send,
    att_recv,
    terms_send,
    terms_recv,
    w_send,
    w_hand,
    w_recv,
    k_send,
    k_hand,
    k_recv,
    v_send,
    v_hand,
    v_recv,
):
    row, col = lax.axis_index("row"), lax.axis_index("col")
    samples, rows, full = tokens_ref.shape
    width = qkvg.shape[2]
    size = full // H
    heads = width // size
    flat = samples * rows

    loads = {}
    for number, (name, source, target) in enumerate(
        (
            ("scale", scale_w_hbm, scale_w),
            ("shift", shift_w_hbm, shift_w),
            ("pair", pair_hbm, pair),
            ("gate", gate_w_hbm, gate_w),
            ("qkvg", qkvg_hbm, qkvg),
            ("out", out_w_hbm, out_w.at[col]),
            ("in", trans_in_hbm, trans_in),
            ("back", trans_out_hbm, trans_out),
        )
    ):
        loads[name] = pltpu.make_async_copy(source, target, load_sem.at[number])
        loads[name].start()

    mods0_x = Exchange("col", n_col, lambda t: mods0.at[col], mods0, mods0_send, mods0_recv)
    mods1_x = Exchange("col", n_col, lambda t: mods1.at[col], mods1, mods1_send, mods1_recv)
    bias_x = Exchange(
        "col", n_col, lambda t: bias_tx.at[pl.ds(t * heads, heads)], bias_rx, bias_send, bias_recv
    )
    att_x = Exchange("col", n_col, lambda t: attended.at[col], attended, att_send, att_recv)
    terms_x = Exchange("col", n_col, lambda t: terms_tx.at[t], terms_rx, terms_send, terms_recv)
    w_x = PairGather("col", n_col, out_w, w_send, w_hand, w_recv)
    k_x = PairGather("row", n_row, keys, k_send, k_hand, k_recv)
    v_x = PairGather("row", n_row, values, v_send, v_hand, v_recv)

    barrier = pltpu.get_barrier_semaphore()
    for d in range(1, n_col):
        pl.semaphore_signal(
            barrier,
            inc=1,
            device_id={"col": lax.rem(col + d, n_col)},
            device_id_type=pl.DeviceIdType.MESH,
        )
    for target in [k_x.mate(d) for d in range(1, n_row // 2)] + [k_x.partner]:
        pl.semaphore_signal(
            barrier, inc=1, device_id={"row": target}, device_id_type=pl.DeviceIdType.MESH
        )

    base = layer_norm(single_ref[...].astype(F32))
    cond0 = (base * ada_gain_ref[0:1, :]).astype(BF16)
    cond1 = (base * ada_gain_ref[1:2, :]).astype(BF16)
    loads["scale"].wait()
    loads["shift"].wait()
    scale0 = jax.nn.sigmoid(dot(cond0, scale_w[0]) + scale_b_ref[0:1, :])
    shift0 = dot(cond0, shift_w[0])
    mods0[col] = jnp.concatenate([scale0, shift0], axis=0).astype(BF16)
    pl.semaphore_wait(barrier, n_col - 1 + n_row // 2)
    mods0_x.start()

    loads["pair"].wait()
    proj = jnp.transpose(pair_proj_ref[...])
    proj_hi = proj.astype(BF16)
    proj_lo = (proj - proj_hi.astype(F32)).astype(BF16)
    proj_both = jnp.concatenate(
        [
            jnp.concatenate([proj_hi, proj_hi], axis=1),
            jnp.concatenate([proj_lo, proj_lo], axis=1),
        ],
        axis=0,
    )
    gain = pair_gain_ref[...]

    def bias_step(step, carry):
        first = pl.multiple_of(step * 8, 8)
        found = []
        for k in range(8):
            normed = layer_norm(pair[first + k]) * gain
            high = normed.astype(BF16)
            low = (normed - high.astype(F32)).astype(BF16)
            both = dot_t(proj_both, jnp.concatenate([high, low], axis=1))
            found.append(both[:H] + both[H:])
        stacked = jnp.stack(found, axis=0)
        bias_tx[:, pl.ds(first, 8), :] = jnp.transpose(stacked, (1, 0, 2))
        return carry

    lax.fori_loop(0, rows // 8, bias_step, 0)
    bias_x.start()

    tokens = tokens_ref[...].astype(F32)
    tokens_normed = layer_norm(tokens)

    def across(parts, first):
        return jnp.concatenate([p[first * rows : (first + 1) * rows] for p in parts], axis=1)

    mods0_x.arrive()
    parts = [mods0[c].astype(F32) for c in range(n_col)]
    norm_in = across(parts, 0)[None] * tokens_normed + across(parts, 1)[None]
    norm_in = norm_in.reshape(flat, full).astype(BF16)
    loads["qkvg"].wait()
    keys[row] = dot(norm_in, qkvg[1]).astype(BF16)
    k_x.start()
    values[row] = dot(norm_in, qkvg[2]).astype(BF16)
    v_x.start()

    loads["gate"].wait()
    gate0 = jax.nn.sigmoid(dot(cond0, gate_w[0]) + gate_b_ref[0:1, :])
    scale1 = jax.nn.sigmoid(dot(cond1, scale_w[1]) + scale_b_ref[1:2, :])
    shift1 = dot(cond1, shift_w[1])
    mods1[col] = jnp.concatenate([gate0, scale1, shift1], axis=0)
    mods1_x.start()
    loads["out"].wait()
    w_x.start()

    query = (dot(norm_in, qkvg[0]) + query_b_ref[...]).astype(BF16).astype(F32)
    gates = jax.nn.sigmoid(dot(norm_in, qkvg[3]))
    gate1 = jax.nn.sigmoid(dot(cond1, gate_w[1]) + gate_b_ref[1:2, :])
    lane = lax.broadcasted_iota(jnp.int32, (rows, width), 1)
    masks = [(lane >= h * size) & (lane < (h + 1) * size) for h in range(heads)]
    bias_rx[col] = bias_tx[pl.ds(col * heads, heads)]
    bias_x.arrive()

    k_x.hand_on()
    v_x.hand_on()
    w_x.hand_on()
    k_x.arrive()
    per_block = n_row // n_col
    weights, totals = [], []
    for s in range(samples):
        span = slice(s * rows, (s + 1) * rows)
        stacked_query = jnp.concatenate(
            [jnp.where(mask, query[span], 0.0) for mask in masks], axis=0
        ).astype(BF16)
        scores = []
        for b in range(n_col):
            block = jnp.concatenate(
                [keys[b * per_block + r].astype(F32)[span] for r in range(per_block)], axis=0
            ).astype(BF16)
            bias = bias_rx[b].reshape(heads * rows, per_block * rows)
            scores.append(dot_t(stacked_query, block) * (1.0 / math.sqrt(size)) + bias)
        peak = functools.reduce(jnp.maximum, scores)
        peak = jnp.max(peak, axis=-1, keepdims=True)
        scores = [jnp.exp(score - peak) for score in scores]
        totals.append(jnp.sum(functools.reduce(jnp.add, scores), axis=-1, keepdims=True))
        weights.append([score.astype(BF16) for score in scores])

    v_x.arrive()
    results = []
    for s in range(samples):
        span = slice(s * rows, (s + 1) * rows)
        accum = jnp.zeros((heads * rows, width), F32)
        for b in range(n_col):
            block = jnp.concatenate(
                [values[b * per_block + r].astype(F32)[span] for r in range(per_block)], axis=0
            ).astype(BF16)
            accum = accum + dot(weights[s][b], block)
        accum = accum / totals[s]
        mine = jnp.zeros((rows, width), F32)
        for h in range(heads):
            mine = jnp.where(masks[h], accum[h * rows : (h + 1) * rows], mine)
        results.append(gates[span] * mine)
    attended[col] = jnp.concatenate(results, axis=0).astype(BF16)
    att_x.start()

    mods1_x.arrive()
    parts = [mods1[c] for c in range(n_col)]
    gate0_all, scale1_all, shift1_all = (across(parts, k)[None] for k in range(3))
    w_x.arrive()
    att_x.arrive()
    projected = jnp.zeros((flat, full), F32)
    for c in range(n_col):
        projected = projected + dot(attended[c], out_w[c])
    resid = tokens + gate0_all * projected.reshape(samples, rows, full)
    middle = (scale1_all * layer_norm(resid) + shift1_all).reshape(flat, full).astype(BF16)
    loads["in"].wait()
    inner = dot(middle, trans_in[0])
    hidden = (jax.nn.silu(inner) * dot(middle, trans_in[1])).astype(BF16)
    loads["back"].wait()
    terms = dot(hidden, trans_out[...])
    for c in range(n_col):
        part = terms[:, c * width : (c + 1) * width]
        terms32[c] = part
        terms_tx[c] = part.astype(BF16)
    terms_x.start()
    resid = resid.reshape(flat, full)
    for c in range(n_col):
        resid_parts[c] = resid[:, c * width : (c + 1) * width]
    outward = terms32[col]
    terms_x.arrive()
    for d in range(1, n_col):
        outward = outward + terms_rx[lax.rem(col + d, n_col)].astype(F32)
    outward = outward.reshape(samples, rows, width)
    mixed = resid_parts[col].reshape(samples, rows, width) + gate1[None] * outward
    out_ref[...] = mixed.astype(BF16)

    for exchange in (mods0_x, bias_x, mods1_x, w_x, k_x, v_x, att_x, terms_x):
        exchange.drain()


def shards(
    n_row,
    n_col,
    tokens,
    single_cond,
    pair_cond,
    ada_gain,
    ada_scale_w,
    ada_scale_b,
    adaptive_shift_weight,
    pair_gain,
    pair_proj,
    qkvg_weight,
    query_bias,
    output_weight,
    out_gate_w,
    out_gate_b,
    transition_input_weight,
    trans_out,
):
    samples, rows, full = tokens.shape
    width = qkvg_weight.shape[2]
    heads = width * H // full
    flat = samples * rows
    keys_here = pair_cond.shape[1]
    vmem = pl.BlockSpec(memory_space=pltpu.VMEM)
    hbm = pl.BlockSpec(memory_space=pl.ANY)

    def like(array):
        return pltpu.VMEM(array.shape, array.dtype)

    def sems(n):
        return pltpu.SemaphoreType.DMA((n,))

    return pl.pallas_call(
        functools.partial(kernel, n_row, n_col),
        out_shape=jax.ShapeDtypeStruct((samples, rows, width), BF16),
        in_specs=[vmem] * 8 + [hbm] * 8,
        out_specs=vmem,
        scratch_shapes=[
            like(ada_scale_w),
            like(adaptive_shift_weight),
            like(pair_cond),
            like(qkvg_weight),
            like(out_gate_w),
            like(transition_input_weight),
            like(trans_out),
            pltpu.VMEM((n_col,) + output_weight.shape, BF16),
            pltpu.VMEM((n_col, 2 * rows, width), BF16),
            pltpu.VMEM((n_col, 3 * rows, width), F32),
            pltpu.VMEM((H, rows, keys_here), F32),
            pltpu.VMEM((n_col, heads, rows, keys_here), F32),
            pltpu.VMEM((n_row, flat, width), BF16),
            pltpu.VMEM((n_row, flat, width), BF16),
            pltpu.VMEM((n_col, flat, width), BF16),
            pltpu.VMEM((n_col, flat, width), F32),
            pltpu.VMEM((n_col, flat, width), BF16),
            pltpu.VMEM((n_col, flat, width), BF16),
            pltpu.VMEM((n_col, flat, width), F32),
            sems(8),
        ]
        + [sems(n_col)] * 10
        + [sems(n_col)] * 3
        + [sems(n_row)] * 6,
        compiler_params=pltpu.CompilerParams(
            collective_id=0, has_side_effects=True, vmem_limit_bytes=56 * 1024 * 1024
        ),
    )(
        tokens,
        single_cond,
        ada_gain,
        ada_scale_b,
        query_bias[None],
        out_gate_b,
        pair_gain[None],
        pair_proj,
        ada_scale_w,
        adaptive_shift_weight,
        pair_cond,
        qkvg_weight,
        out_gate_w,
        output_weight,
        transition_input_weight,
        trans_out,
    )


def solution(mesh):
    return jax.shard_map(
        functools.partial(shards, mesh.shape["row"], mesh.shape["col"]),
        mesh=mesh,
        in_specs=(
            P(None, "row", None),
            P("row", None),
            P("row", "col", None),
            P(),
            P(None, None, "col"),
            P(None, "col"),
            P(None, None, "col"),
            P(),
            P(),
            P(None, None, "col"),
            P("col"),
            P("col", None),
            P(None, None, "col"),
            P(None, "col"),
            P(None, None, "col"),
            P("col", None),
        ),
        out_specs=P(None, "row", "col"),
        check_vma=False,
    )
```

```python
import functools
import math

import jax
import jax.numpy as jnp
from jax import lax
from jax.experimental import pallas as pl
from jax.experimental.pallas import tpu as pltpu
from jax.sharding import PartitionSpec as P

H = 16
epsilon = 1e-05
F32 = jnp.float32
BF16 = jnp.bfloat16


def layer_norm(values):
    center = values - jnp.mean(values, axis=-1, keepdims=True)
    spread = jnp.mean(center * center, axis=-1, keepdims=True)
    return center * lax.rsqrt(spread + epsilon)


def dot(a, b):
    return jnp.dot(a, b, preferred_element_type=F32)


def dot_t(a, b):
    return lax.dot_general(a, b, (((1,), (1,)), ((), ())), preferred_element_type=F32)


class Exchange:
    def __init__(self, axis, n, source, buffer, send, recv):
        self.axis, self.n, self.source, self.buffer = axis, n, source, buffer
        self.send, self.recv = send, recv
        self.me = lax.axis_index(axis)

    def copy(self, d):
        target = lax.rem(self.me + d, self.n)
        return pltpu.make_async_remote_copy(
            src_ref=self.source(target),
            dst_ref=self.buffer.at[self.me],
            send_sem=self.send.at[d],
            recv_sem=self.recv.at[self.me],
            device_id={self.axis: target},
            device_id_type=pl.DeviceIdType.MESH,
        )

    def start(self):
        for d in range(1, self.n):
            self.copy(d).start()

    def arrive(self):
        for d in range(1, self.n):
            origin = lax.rem(self.me + d, self.n)
            pltpu.make_async_remote_copy(
                src_ref=self.buffer.at[origin],
                dst_ref=self.buffer.at[origin],
                send_sem=self.send.at[d],
                recv_sem=self.recv.at[origin],
                device_id={self.axis: origin},
                device_id_type=pl.DeviceIdType.MESH,
            ).wait_recv()

    def drain(self):
        for d in range(1, self.n):
            self.copy(d).wait_send()


class PairGather:
    def __init__(self, axis, n, buffer, send, handed, recv):
        self.axis, self.n, self.buffer = axis, n, buffer
        self.send, self.handed, self.recv = send, handed, recv
        self.me = lax.axis_index(axis)
        self.partner = self.me + 1 - 2 * lax.rem(self.me, 2)

    def copy(self, block, target, sem):
        return pltpu.make_async_remote_copy(
            src_ref=self.buffer.at[block],
            dst_ref=self.buffer.at[block],
            send_sem=sem,
            recv_sem=self.recv.at[block],
            device_id={self.axis: target},
            device_id_type=pl.DeviceIdType.MESH,
        )

    def mate(self, d):
        return lax.rem(self.me + 2 * d, self.n)

    def start(self):
        for d in range(1, self.n // 2):
            self.copy(self.me, self.mate(d), self.send.at[d]).start()
        self.copy(self.me, self.partner, self.send.at[0]).start()

    def hand_on(self):
        for d in range(1, self.n // 2):
            block = self.mate(d)
            self.copy(block, self.partner, self.handed.at[d]).wait_recv()
            self.copy(block, self.partner, self.handed.at[d]).start()

    def arrive(self):
        for d in range(self.n // 2):
            block = lax.rem(self.partner + 2 * d, self.n)
            self.copy(block, self.partner, self.send.at[0]).wait_recv()

    def drain(self):
        for d in range(1, self.n // 2):
            self.copy(self.me, self.mate(d), self.send.at[d]).wait_send()
            self.copy(self.mate(d), self.partner, self.handed.at[d]).wait_send()
        self.copy(self.me, self.partner, self.send.at[0]).wait_send()


def kernel(
    n_row,
    n_col,
    tokens_ref,
    single_ref,
    ada_gain_ref,
    scale_b_ref,
    query_b_ref,
    gate_b_ref,
    pair_gain_ref,
    pair_proj_ref,
    scale_w_hbm,
    shift_w_hbm,
    pair_hbm,
    qkvg_hbm,
    gate_w_hbm,
    out_w_hbm,
    trans_in_hbm,
    trans_out_hbm,
    out_ref,
    scale_w,
    shift_w,
    pair,
    qkvg,
    gate_w,
    trans_in,
    trans_out,
    out_w,
    mods0,
    mods1,
    bias_tx,
    bias_rx,
    keys,
    values,
    attended,
    terms32,
    terms_tx,
    terms_rx,
    resid_parts,
    load_sem,
    mods0_send,
    mods0_recv,
    mods1_send,
    mods1_recv,
    bias_send,
    bias_recv,
    att_send,
    att_recv,
    terms_send,
    terms_recv,
    w_send,
    w_hand,
    w_recv,
    k_send,
    k_hand,
    k_recv,
    v_send,
    v_hand,
    v_recv,
):
    row, col = lax.axis_index("row"), lax.axis_index("col")
    samples, rows, full = tokens_ref.shape
    width = qkvg.shape[1]
    size = full // H
    heads = width // size
    flat = samples * rows

    loads = {}
    for number, (name, source, target) in enumerate(
        (
            ("scale", scale_w_hbm, scale_w),
            ("shift", shift_w_hbm, shift_w),
            ("pair", pair_hbm, pair),
            ("gate", gate_w_hbm, gate_w),
            ("qkvg", qkvg_hbm, qkvg),
            ("out", out_w_hbm, out_w.at[col]),
            ("in", trans_in_hbm, trans_in),
            ("back", trans_out_hbm, trans_out),
        )
    ):
        loads[name] = pltpu.make_async_copy(source, target, load_sem.at[number])
        loads[name].start()

    mods0_x = Exchange("col", n_col, lambda t: mods0.at[col], mods0, mods0_send, mods0_recv)
    mods1_x = Exchange("col", n_col, lambda t: mods1.at[col], mods1, mods1_send, mods1_recv)
    bias_x = Exchange(
        "col", n_col, lambda t: bias_tx.at[pl.ds(t * heads, heads)], bias_rx, bias_send, bias_recv
    )
    att_x = Exchange("col", n_col, lambda t: attended.at[col], attended, att_send, att_recv)
    terms_x = Exchange("col", n_col, lambda t: terms_tx.at[t], terms_rx, terms_send, terms_recv)
    w_x = PairGather("col", n_col, out_w, w_send, w_hand, w_recv)
    k_x = PairGather("row", n_row, keys, k_send, k_hand, k_recv)
    v_x = PairGather("row", n_row, values, v_send, v_hand, v_recv)

    barrier = pltpu.get_barrier_semaphore()
    for d in range(1, n_col):
        pl.semaphore_signal(
            barrier,
            inc=1,
            device_id={"col": lax.rem(col + d, n_col)},
            device_id_type=pl.DeviceIdType.MESH,
        )
    for target in [k_x.mate(d) for d in range(1, n_row // 2)] + [k_x.partner]:
        pl.semaphore_signal(
            barrier, inc=1, device_id={"row": target}, device_id_type=pl.DeviceIdType.MESH
        )

    base = layer_norm(single_ref[...].astype(F32))
    cond0 = (base * ada_gain_ref[0:1, :]).astype(BF16)
    cond1 = (base * ada_gain_ref[1:2, :]).astype(BF16)
    loads["scale"].wait()
    loads["shift"].wait()
    scale0 = jax.nn.sigmoid(dot_t(cond0, scale_w[0]) + scale_b_ref[0:1, :])
    shift0 = dot_t(cond0, shift_w[0])
    mods0[col] = jnp.concatenate([scale0, shift0], axis=0).astype(BF16)
    pl.semaphore_wait(barrier, n_col - 1 + n_row // 2)
    mods0_x.start()

    loads["pair"].wait()
    proj = pair_proj_ref[...]
    proj_hi = proj.astype(BF16)
    proj_lo = (proj - proj_hi.astype(F32)).astype(BF16)
    proj_both = jnp.concatenate(
        [
            jnp.concatenate([proj_hi, proj_hi], axis=1),
            jnp.concatenate([proj_lo, proj_lo], axis=1),
        ],
        axis=0,
    )
    gain = pair_gain_ref[...]

    def bias_step(step, carry):
        first = pl.multiple_of(step * 8, 8)
        found = []
        for k in range(8):
            normed = layer_norm(pair[first + k]) * gain
            high = normed.astype(BF16)
            low = (normed - high.astype(F32)).astype(BF16)
            both = dot_t(proj_both, jnp.concatenate([high, low], axis=1))
            found.append(both[:H] + both[H:])
        stacked = jnp.stack(found, axis=0)
        bias_tx[:, pl.ds(first, 8), :] = jnp.transpose(stacked, (1, 0, 2))
        return carry

    lax.fori_loop(0, rows // 8, bias_step, 0)
    bias_x.start()

    tokens = tokens_ref[...].astype(F32)
    tokens_normed = layer_norm(tokens)

    def across(parts, first):
        return jnp.concatenate([p[first * rows : (first + 1) * rows] for p in parts], axis=1)

    mods0_x.arrive()
    parts = [mods0[c].astype(F32) for c in range(n_col)]
    norm_in = across(parts, 0)[None] * tokens_normed + across(parts, 1)[None]
    norm_in = norm_in.reshape(flat, full).astype(BF16)
    loads["qkvg"].wait()
    keys[row] = dot_t(norm_in, qkvg[1]).astype(BF16)
    k_x.start()
    values[row] = dot_t(norm_in, qkvg[2]).astype(BF16)
    v_x.start()

    loads["gate"].wait()
    gate0 = jax.nn.sigmoid(dot_t(cond0, gate_w[0]) + gate_b_ref[0:1, :])
    scale1 = jax.nn.sigmoid(dot_t(cond1, scale_w[1]) + scale_b_ref[1:2, :])
    shift1 = dot_t(cond1, shift_w[1])
    mods1[col] = jnp.concatenate([gate0, scale1, shift1], axis=0)
    mods1_x.start()
    loads["out"].wait()
    w_x.start()

    query = (dot_t(norm_in, qkvg[0]) + query_b_ref[...]).astype(BF16).astype(F32)
    gates = jax.nn.sigmoid(dot_t(norm_in, qkvg[3]))
    gate1 = jax.nn.sigmoid(dot_t(cond1, gate_w[1]) + gate_b_ref[1:2, :])
    lane = lax.broadcasted_iota(jnp.int32, (rows, width), 1)
    masks = [(lane >= h * size) & (lane < (h + 1) * size) for h in range(heads)]
    bias_rx[col] = bias_tx[pl.ds(col * heads, heads)]
    bias_x.arrive()

    k_x.hand_on()
    v_x.hand_on()
    w_x.hand_on()
    k_x.arrive()
    per_block = n_row // n_col
    weights, totals = [], []
    for s in range(samples):
        span = slice(s * rows, (s + 1) * rows)
        stacked_query = jnp.concatenate(
            [jnp.where(mask, query[span], 0.0) for mask in masks], axis=0
        ).astype(BF16)
        scores = []
        for b in range(n_col):
            block = jnp.concatenate(
                [keys[b * per_block + r].astype(F32)[span] for r in range(per_block)], axis=0
            ).astype(BF16)
            bias = bias_rx[b].reshape(heads * rows, per_block * rows)
            scores.append(dot_t(stacked_query, block) * (1.0 / math.sqrt(size)) + bias)
        peak = functools.reduce(jnp.maximum, scores)
        peak = jnp.max(peak, axis=-1, keepdims=True)
        scores = [jnp.exp(score - peak) for score in scores]
        totals.append(jnp.sum(functools.reduce(jnp.add, scores), axis=-1, keepdims=True))
        weights.append([score.astype(BF16) for score in scores])

    v_x.arrive()
    results = []
    for s in range(samples):
        span = slice(s * rows, (s + 1) * rows)
        accum = jnp.zeros((heads * rows, width), F32)
        for b in range(n_col):
            block = jnp.concatenate(
                [values[b * per_block + r].astype(F32)[span] for r in range(per_block)], axis=0
            ).astype(BF16)
            accum = accum + dot(weights[s][b], block)
        accum = accum / totals[s]
        mine = jnp.zeros((rows, width), F32)
        for h in range(heads):
            mine = jnp.where(masks[h], accum[h * rows : (h + 1) * rows], mine)
        results.append(gates[span] * mine)
    attended[col] = jnp.concatenate(results, axis=0).astype(BF16)
    att_x.start()

    mods1_x.arrive()
    parts = [mods1[c] for c in range(n_col)]
    gate0_all, scale1_all, shift1_all = (across(parts, k)[None] for k in range(3))
    w_x.arrive()
    att_x.arrive()
    projected = jnp.zeros((flat, full), F32)
    for c in range(n_col):
        projected = projected + dot(attended[c], out_w[c])
    resid = tokens + gate0_all * projected.reshape(samples, rows, full)
    middle = (scale1_all * layer_norm(resid) + shift1_all).reshape(flat, full).astype(BF16)
    loads["in"].wait()
    inner = dot(middle, trans_in[0])
    hidden = (jax.nn.silu(inner) * dot(middle, trans_in[1])).astype(BF16)
    loads["back"].wait()
    terms = dot(hidden, trans_out[...])
    for c in range(n_col):
        part = terms[:, c * width : (c + 1) * width]
        terms32[c] = part
        terms_tx[c] = part.astype(BF16)
    terms_x.start()
    resid = resid.reshape(flat, full)
    for c in range(n_col):
        resid_parts[c] = resid[:, c * width : (c + 1) * width]
    outward = terms32[col]
    terms_x.arrive()
    for d in range(1, n_col):
        outward = outward + terms_rx[lax.rem(col + d, n_col)].astype(F32)
    outward = outward.reshape(samples, rows, width)
    mixed = resid_parts[col].reshape(samples, rows, width) + gate1[None] * outward
    out_ref[...] = mixed

    for exchange in (mods0_x, bias_x, mods1_x, w_x, k_x, v_x, att_x, terms_x):
        exchange.drain()


def shards(
    n_row,
    n_col,
    tokens,
    single_cond,
    pair_cond,
    ada_gain,
    ada_scale_w,
    ada_scale_b,
    adaptive_shift_weight,
    pair_gain,
    pair_proj,
    qkvg_weight,
    query_bias,
    output_weight,
    out_gate_w,
    out_gate_b,
    transition_input_weight,
    trans_out,
):
    samples, rows, full = tokens.shape
    width = qkvg_weight.shape[2]
    heads = width * H // full
    flat = samples * rows
    keys_here = pair_cond.shape[1]
    ada_scale_w, adaptive_shift_weight, qkvg_weight, out_gate_w = (
        jnp.swapaxes(array, 1, 2)
        for array in (ada_scale_w, adaptive_shift_weight, qkvg_weight, out_gate_w)
    )
    vmem = pl.BlockSpec(memory_space=pltpu.VMEM)
    hbm = pl.BlockSpec(memory_space=pl.ANY)

    def like(array):
        return pltpu.VMEM(array.shape, array.dtype)

    def sems(n):
        return pltpu.SemaphoreType.DMA((n,))

    mixed = pl.pallas_call(
        functools.partial(kernel, n_row, n_col),
        out_shape=jax.ShapeDtypeStruct((samples, rows, width), F32),
        in_specs=[vmem] * 8 + [hbm] * 8,
        out_specs=vmem,
        scratch_shapes=[
            like(ada_scale_w),
            like(adaptive_shift_weight),
            like(pair_cond),
            like(qkvg_weight),
            like(out_gate_w),
            like(transition_input_weight),
            like(trans_out),
            pltpu.VMEM((n_col,) + output_weight.shape, BF16),
            pltpu.VMEM((n_col, 2 * rows, width), BF16),
            pltpu.VMEM((n_col, 3 * rows, width), F32),
            pltpu.VMEM((H, rows, keys_here), F32),
            pltpu.VMEM((n_col, heads, rows, keys_here), F32),
            pltpu.VMEM((n_row, flat, width), BF16),
            pltpu.VMEM((n_row, flat, width), BF16),
            pltpu.VMEM((n_col, flat, width), BF16),
            pltpu.VMEM((n_col, flat, width), F32),
            pltpu.VMEM((n_col, flat, width), BF16),
            pltpu.VMEM((n_col, flat, width), BF16),
            pltpu.VMEM((n_col, flat, width), F32),
            sems(8),
        ]
        + [sems(n_col)] * 10
        + [sems(n_col)] * 3
        + [sems(n_row)] * 6,
        compiler_params=pltpu.CompilerParams(
            collective_id=0, has_side_effects=True, vmem_limit_bytes=56 * 1024 * 1024
        ),
    )(
        tokens,
        single_cond,
        ada_gain,
        ada_scale_b,
        query_bias[None],
        out_gate_b,
        pair_gain[None],
        pair_proj.T,
        ada_scale_w,
        adaptive_shift_weight,
        pair_cond,
        qkvg_weight,
        out_gate_w,
        output_weight,
        transition_input_weight,
        trans_out,
    )
    return mixed.astype(BF16)


def solution(mesh):
    return jax.shard_map(
        functools.partial(shards, mesh.shape["row"], mesh.shape["col"]),
        mesh=mesh,
        in_specs=(
            P(None, "row", None),
            P("row", None),
            P("row", "col", None),
            P(),
            P(None, None, "col"),
            P(None, "col"),
            P(None, None, "col"),
            P(),
            P(),
            P(None, None, "col"),
            P("col"),
            P("col", None),
            P(None, None, "col"),
            P(None, "col"),
            P(None, None, "col"),
            P("col", None),
        ),
        out_specs=P(None, "row", "col"),
        check_vma=False,
    )
```

```python
import functools
import math

import jax
import jax.numpy as jnp
from jax import lax
from jax.experimental import pallas as pl
from jax.experimental.pallas import tpu as pltpu
from jax.sharding import PartitionSpec as P

H = 16
PARTS = 2
epsilon = 1e-05
F32 = jnp.float32
BF16 = jnp.bfloat16


def layer_norm(values):
    center = values - jnp.mean(values, axis=-1, keepdims=True)
    spread = jnp.mean(center * center, axis=-1, keepdims=True)
    return center * lax.rsqrt(spread + epsilon)


def dot(a, b):
    return jnp.dot(a, b, preferred_element_type=F32)


def dot_t(a, b):
    return lax.dot_general(a, b, (((1,), (1,)), ((), ())), preferred_element_type=F32)


class Exchange:
    def __init__(self, axis, n, source, buffer, send, recv):
        self.axis, self.n, self.source, self.buffer = axis, n, source, buffer
        self.send, self.recv = send, recv
        self.me = lax.axis_index(axis)

    def copy(self, d):
        target = lax.rem(self.me + d, self.n)
        return pltpu.make_async_remote_copy(
            src_ref=self.source(target),
            dst_ref=self.buffer.at[self.me],
            send_sem=self.send.at[d],
            recv_sem=self.recv.at[self.me],
            device_id={self.axis: target},
            device_id_type=pl.DeviceIdType.MESH,
        )

    def start(self):
        for d in range(1, self.n):
            self.copy(d).start()

    def arrive(self):
        for d in range(1, self.n):
            origin = lax.rem(self.me + d, self.n)
            pltpu.make_async_remote_copy(
                src_ref=self.buffer.at[origin],
                dst_ref=self.buffer.at[origin],
                send_sem=self.send.at[d],
                recv_sem=self.recv.at[origin],
                device_id={self.axis: origin},
                device_id_type=pl.DeviceIdType.MESH,
            ).wait_recv()

    def drain(self):
        for d in range(1, self.n):
            self.copy(d).wait_send()


class PairGather:
    def __init__(self, axis, n, buffer, send, handed, recv):
        self.axis, self.n, self.buffer = axis, n, buffer
        self.send, self.handed, self.recv = send, handed, recv
        self.me = lax.axis_index(axis)
        self.partner = self.me + 1 - 2 * lax.rem(self.me, 2)

    def copy(self, block, target, sem):
        return pltpu.make_async_remote_copy(
            src_ref=self.buffer.at[block],
            dst_ref=self.buffer.at[block],
            send_sem=sem,
            recv_sem=self.recv.at[block],
            device_id={self.axis: target},
            device_id_type=pl.DeviceIdType.MESH,
        )

    def mate(self, d):
        return lax.rem(self.me + 2 * d, self.n)

    def start(self):
        for d in range(1, self.n // 2):
            self.copy(self.me, self.mate(d), self.send.at[d]).start()
        self.copy(self.me, self.partner, self.send.at[0]).start()

    def hand_on(self):
        for d in range(1, self.n // 2):
            block = self.mate(d)
            self.copy(block, self.partner, self.handed.at[d]).wait_recv()
            self.copy(block, self.partner, self.handed.at[d]).start()

    def arrive(self):
        for d in range(self.n // 2):
            block = lax.rem(self.partner + 2 * d, self.n)
            self.copy(block, self.partner, self.send.at[0]).wait_recv()

    def drain(self):
        for d in range(1, self.n // 2):
            self.copy(self.me, self.mate(d), self.send.at[d]).wait_send()
            self.copy(self.mate(d), self.partner, self.handed.at[d]).wait_send()
        self.copy(self.me, self.partner, self.send.at[0]).wait_send()


class LineGather:
    def __init__(self, axis, n, buffer, send, handed, recv):
        self.axis, self.n, self.buffer = axis, n, buffer
        self.send, self.handed, self.recv = send, handed, recv
        self.me = lax.axis_index(axis)
        self.side = lax.rem(self.me, 2)
        self.place = self.me // 2
        self.length = n // 2
        self.partner = self.me + 1 - 2 * self.side

    def copy(self, block, target, sem):
        return pltpu.make_async_remote_copy(
            src_ref=self.buffer.at[block],
            dst_ref=self.buffer.at[block],
            send_sem=sem,
            recv_sem=self.recv.at[block],
            device_id={self.axis: target},
            device_id_type=pl.DeviceIdType.MESH,
        )

    def upward(self, k):
        return self.copy(self.me - 2 * k, self.me + 2, self.send.at[k])

    def downward(self, k):
        return self.copy(self.me + 2 * k, self.me - 2, self.send.at[self.length + k])

    def from_below(self, k):
        return self.copy(self.me - 2 * k, self.partner, self.handed.at[k])

    def from_above(self, k):
        return self.copy(self.me + 2 * k, self.partner, self.handed.at[self.length + k])

    def start(self):
        pl.when(self.place < self.length - 1)(lambda: self.upward(0).start())
        pl.when(self.place > 0)(lambda: self.downward(0).start())
        self.from_below(0).start()

    def step(self, k):
        @pl.when(self.place >= k)
        def _():
            self.from_below(k).wait_recv()
            pl.when(self.place < self.length - 1)(lambda: self.upward(k).start())
            self.from_below(k).start()

        @pl.when(self.place < self.length - k)
        def _():
            self.from_above(k).wait_recv()
            pl.when(self.place > 0)(lambda: self.downward(k).start())
            self.from_above(k).start()

    def arrive(self):
        for d in range(self.length):
            self.copy(2 * d + 1 - self.side, self.partner, self.send.at[0]).wait_recv()

    def drain(self):
        self.from_below(0).wait_send()
        for k in range(self.length):
            below = self.place >= k
            above = self.place < self.length - k
            last = self.place == self.length - 1
            first = self.place == 0
            pl.when(below & ~last)(lambda k=k: self.upward(k).wait_send())
            pl.when(above & ~first)(lambda k=k: self.downward(k).wait_send())
            if k:
                pl.when(below)(lambda k=k: self.from_below(k).wait_send())
                pl.when(above)(lambda k=k: self.from_above(k).wait_send())


def kernel(
    n_row,
    n_col,
    tokens_ref,
    single_ref,
    ada_gain_ref,
    scale_b_ref,
    query_b_ref,
    gate_b_ref,
    pair_gain_ref,
    pair_proj_ref,
    scale_w_hbm,
    shift_w_hbm,
    pair_hbm,
    qkvg_hbm,
    gate_w_hbm,
    out_w_hbm,
    trans_in_hbm,
    trans_out_hbm,
    out_ref,
    scale_w,
    shift_w,
    pair,
    qkvg,
    gate_w,
    trans_in,
    trans_out,
    out_w,
    mods0,
    mods1,
    bias_tx,
    bias_rx,
    kv,
    attended,
    terms32,
    terms_tx,
    terms_rx,
    resid_parts,
    load_sem,
    mods0_send,
    mods0_recv,
    mods1_send,
    mods1_recv,
    bias_send,
    bias_recv,
    att_send,
    att_recv,
    terms_send,
    terms_recv,
    w_send,
    w_hand,
    w_recv,
    kv_send,
    kv_hand,
    kv_recv,
):
    row, col = lax.axis_index("row"), lax.axis_index("col")
    samples, rows, full = tokens_ref.shape
    width = qkvg.shape[1]
    size = full // H
    heads = width // size
    flat = samples * rows
    some = samples // PARTS
    part_flat = flat // PARTS

    loads = {}
    for number, (name, source, target) in enumerate(
        (
            ("scale", scale_w_hbm, scale_w),
            ("shift", shift_w_hbm, shift_w),
            ("pair", pair_hbm, pair),
            ("gate", gate_w_hbm, gate_w),
            ("qkvg", qkvg_hbm, qkvg),
            ("out", out_w_hbm, out_w.at[col]),
            ("in", trans_in_hbm, trans_in),
            ("back", trans_out_hbm, trans_out),
        )
    ):
        loads[name] = pltpu.make_async_copy(source, target, load_sem.at[number])
        loads[name].start()

    mods0_x = Exchange("col", n_col, lambda t: mods0.at[col], mods0, mods0_send, mods0_recv)
    mods1_x = Exchange("col", n_col, lambda t: mods1.at[col], mods1, mods1_send, mods1_recv)
    bias_x = Exchange(
        "col", n_col, lambda t: bias_tx.at[pl.ds(t * heads, heads)], bias_rx, bias_send, bias_recv
    )
    att_x = Exchange("col", n_col, lambda t: attended.at[col], attended, att_send, att_recv)
    terms_x = Exchange("col", n_col, lambda t: terms_tx.at[t], terms_rx, terms_send, terms_recv)
    w_x = PairGather("col", n_col, out_w, w_send, w_hand, w_recv)
    kv_x = [
        LineGather("row", n_row, kv.at[g], kv_send.at[g], kv_hand.at[g], kv_recv.at[g])
        for g in range(PARTS)
    ]

    barrier = pltpu.get_barrier_semaphore()
    for d in range(1, n_col):
        pl.semaphore_signal(
            barrier,
            inc=1,
            device_id={"col": lax.rem(col + d, n_col)},
            device_id_type=pl.DeviceIdType.MESH,
        )
    for target in [lax.rem(row + 2 * d, n_row) for d in range(1, n_row // 2)] + [kv_x[0].partner]:
        pl.semaphore_signal(
            barrier, inc=1, device_id={"row": target}, device_id_type=pl.DeviceIdType.MESH
        )

    base = layer_norm(single_ref[...].astype(F32))
    cond0 = (base * ada_gain_ref[0:1, :]).astype(BF16)
    cond1 = (base * ada_gain_ref[1:2, :]).astype(BF16)
    loads["scale"].wait()
    loads["shift"].wait()
    scale0 = jax.nn.sigmoid(dot_t(cond0, scale_w[0]) + scale_b_ref[0:1, :])
    shift0 = dot_t(cond0, shift_w[0])
    mods0[col] = jnp.concatenate([scale0, shift0], axis=0).astype(BF16)
    pl.semaphore_wait(barrier, n_col - 1 + n_row // 2)
    mods0_x.start()

    loads["pair"].wait()
    proj = pair_proj_ref[...]
    proj_hi = proj.astype(BF16)
    proj_lo = (proj - proj_hi.astype(F32)).astype(BF16)
    proj_both = jnp.concatenate(
        [
            jnp.concatenate([proj_hi, proj_hi], axis=1),
            jnp.concatenate([proj_lo, proj_lo], axis=1),
        ],
        axis=0,
    )
    gain = pair_gain_ref[...]

    def bias_step(step, carry):
        first = pl.multiple_of(step * 8, 8)
        found = []
        for k in range(8):
            normed = layer_norm(pair[first + k]) * gain
            high = normed.astype(BF16)
            low = (normed - high.astype(F32)).astype(BF16)
            both = dot_t(proj_both, jnp.concatenate([high, low], axis=1))
            found.append(both[:H] + both[H:])
        stacked = jnp.stack(found, axis=0)
        bias_tx[:, pl.ds(first, 8), :] = jnp.transpose(stacked, (1, 0, 2))
        return carry

    lax.fori_loop(0, rows // 8, bias_step, 0)
    bias_x.start()

    tokens = tokens_ref[...].astype(F32)
    tokens_normed = layer_norm(tokens)

    def across(parts, first):
        return jnp.concatenate([p[first * rows : (first + 1) * rows] for p in parts], axis=1)

    mods0_x.arrive()
    parts = [mods0[c].astype(F32) for c in range(n_col)]
    norm_in = across(parts, 0)[None] * tokens_normed + across(parts, 1)[None]
    norm_in = norm_in.reshape(flat, full).astype(BF16)
    loads["qkvg"].wait()
    key = dot_t(norm_in, qkvg[1])
    value = dot_t(norm_in, qkvg[2])
    for g in range(PARTS):
        span = slice(g * part_flat, (g + 1) * part_flat)
        kv[g, row] = jnp.concatenate([key[span], value[span]], axis=1).astype(BF16)
    kv_x[0].start()

    loads["gate"].wait()
    gate0 = jax.nn.sigmoid(dot_t(cond0, gate_w[0]) + gate_b_ref[0:1, :])
    scale1 = jax.nn.sigmoid(dot_t(cond1, scale_w[1]) + scale_b_ref[1:2, :])
    shift1 = dot_t(cond1, shift_w[1])
    fill = jnp.zeros((mods1.shape[1] - 3 * rows, width), F32)
    mods1[col] = jnp.concatenate([gate0, scale1, shift1, fill], axis=0).astype(BF16)
    mods1_x.start()
    loads["out"].wait()
    w_x.start()

    query = (dot_t(norm_in, qkvg[0]) + query_b_ref[...]).astype(BF16).astype(F32)
    gates = jax.nn.sigmoid(dot_t(norm_in, qkvg[3]))
    gate1 = jax.nn.sigmoid(dot_t(cond1, gate_w[1]) + gate_b_ref[1:2, :])
    lane = lax.broadcasted_iota(jnp.int32, (rows, width), 1)
    masks = [(lane >= h * size) & (lane < (h + 1) * size) for h in range(heads)]
    bias_rx[col] = bias_tx[pl.ds(col * heads, heads)]
    bias_x.arrive()
    per_block = n_row // n_col

    half = flat // 2

    def pack(array):
        return jnp.concatenate([array[:half], array[half:]], axis=1)

    def unpack(array):
        return jnp.concatenate([array[:, :width], array[:, width:]], axis=0)

    def tokens_of(g, which, b, s):
        lanes = slice(which * width, (which + 1) * width)
        return jnp.concatenate(
            [
                kv[g, b * per_block + r].astype(F32)[s * rows : (s + 1) * rows, lanes]
                for r in range(per_block)
            ],
            axis=0,
        ).astype(BF16)

    def attend(g):
        results = []
        for s in range(some):
            span = slice((g * some + s) * rows, (g * some + s + 1) * rows)
            stacked_query = jnp.concatenate(
                [jnp.where(mask, query[span], 0.0) for mask in masks], axis=0
            ).astype(BF16)
            scores = []
            for b in range(n_col):
                bias = bias_rx[b].reshape(heads * rows, per_block * rows)
                score = dot_t(stacked_query, tokens_of(g, 0, b, s))
                scores.append(score * (1.0 / math.sqrt(size)) + bias)
            peak = functools.reduce(jnp.maximum, scores)
            peak = jnp.max(peak, axis=-1, keepdims=True)
            scores = [jnp.exp(score - peak) for score in scores]
            total = jnp.sum(functools.reduce(jnp.add, scores), axis=-1, keepdims=True)
            accum = jnp.zeros((heads * rows, width), F32)
            for b in range(n_col):
                accum = accum + dot(scores[b].astype(BF16), tokens_of(g, 1, b, s))
            accum = accum / total
            mine = jnp.zeros((rows, width), F32)
            for h in range(heads):
                mine = jnp.where(masks[h], accum[h * rows : (h + 1) * rows], mine)
            results.append(gates[span] * mine)
        return results

    first, second = kv_x
    steps = n_row // 2
    for k in range(1, steps):
        first.step(k)
        if k == 1:
            second.start()
        else:
            second.step(k - 1)
    second.step(steps - 1)
    w_x.hand_on()
    first.arrive()
    results = attend(0)
    second.arrive()
    results = results + attend(1)
    attended[col] = pack(jnp.concatenate(results, axis=0)).astype(BF16)
    att_x.start()
    mods1_x.arrive()
    parts = [mods1[c].astype(F32) for c in range(n_col)]
    gate0_all, scale1_all, shift1_all = (across(parts, k)[None] for k in range(3))
    w_x.arrive()
    loads["in"].wait()
    loads["back"].wait()
    att_x.arrive()
    projected = jnp.zeros((flat, full), F32)
    for c in range(n_col):
        projected = projected + dot(unpack(attended[c].astype(F32)).astype(BF16), out_w[c])
    resid = tokens + gate0_all * projected.reshape(samples, rows, full)
    middle = (scale1_all * layer_norm(resid) + shift1_all).reshape(flat, full).astype(BF16)
    inner = dot(middle, trans_in[0])
    hidden = (jax.nn.silu(inner) * dot(middle, trans_in[1])).astype(BF16)
    terms = dot(hidden, trans_out[...])
    for c in range(n_col):
        part = pack(terms[:, c * width : (c + 1) * width])
        terms32[c] = part
        terms_tx[c] = part.astype(BF16)
    terms_x.start()
    resid = resid.reshape(flat, full)
    for c in range(n_col):
        resid_parts[c] = resid[:, c * width : (c + 1) * width]
    outward = terms32[col]
    terms_x.arrive()
    for d in range(1, n_col):
        outward = outward + terms_rx[lax.rem(col + d, n_col)].astype(F32)
    outward = unpack(outward).reshape(samples, rows, width)
    mixed = resid_parts[col].reshape(samples, rows, width) + gate1[None] * outward
    out_ref[...] = mixed

    for exchange in [mods0_x, bias_x, mods1_x, w_x, att_x, terms_x] + kv_x:
        exchange.drain()


def shards(
    n_row,
    n_col,
    tokens,
    single_cond,
    pair_cond,
    ada_gain,
    ada_scale_w,
    ada_scale_b,
    adaptive_shift_weight,
    pair_gain,
    pair_proj,
    qkvg_weight,
    query_bias,
    output_weight,
    out_gate_w,
    out_gate_b,
    transition_input_weight,
    trans_out,
):
    samples, rows, full = tokens.shape
    width = qkvg_weight.shape[2]
    heads = width * H // full
    flat = samples * rows
    keys_here = pair_cond.shape[1]
    ada_scale_w, adaptive_shift_weight, qkvg_weight, out_gate_w = (
        jnp.swapaxes(array, 1, 2)
        for array in (ada_scale_w, adaptive_shift_weight, qkvg_weight, out_gate_w)
    )
    vmem = pl.BlockSpec(memory_space=pltpu.VMEM)
    hbm = pl.BlockSpec(memory_space=pl.ANY)

    def like(array):
        return pltpu.VMEM(array.shape, array.dtype)

    def sems(*shape):
        return pltpu.SemaphoreType.DMA(shape)

    mixed = pl.pallas_call(
        functools.partial(kernel, n_row, n_col),
        out_shape=jax.ShapeDtypeStruct((samples, rows, width), F32),
        in_specs=[vmem] * 8 + [hbm] * 8,
        out_specs=vmem,
        scratch_shapes=[
            like(ada_scale_w),
            like(adaptive_shift_weight),
            like(pair_cond),
            like(qkvg_weight),
            like(out_gate_w),
            like(transition_input_weight),
            like(trans_out),
            pltpu.VMEM((n_col,) + output_weight.shape, BF16),
            pltpu.VMEM((n_col, 2 * rows, width), BF16),
            pltpu.VMEM((n_col, -(-3 * rows // 16) * 16, width), BF16),
            pltpu.VMEM((H, rows, keys_here), F32),
            pltpu.VMEM((n_col, heads, rows, keys_here), F32),
            pltpu.VMEM((PARTS, n_row, flat // PARTS, 2 * width), BF16),
            pltpu.VMEM((n_col, flat // 2, 2 * width), BF16),
            pltpu.VMEM((n_col, flat // 2, 2 * width), F32),
            pltpu.VMEM((n_col, flat // 2, 2 * width), BF16),
            pltpu.VMEM((n_col, flat // 2, 2 * width), BF16),
            pltpu.VMEM((n_col, flat, width), F32),
            sems(8),
        ]
        + [sems(n_col)] * 13
        + [sems(PARTS, n_row)] * 3,
        compiler_params=pltpu.CompilerParams(
            collective_id=0, has_side_effects=True, vmem_limit_bytes=56 * 1024 * 1024
        ),
    )(
        tokens,
        single_cond,
        ada_gain,
        ada_scale_b,
        query_bias[None],
        out_gate_b,
        pair_gain[None],
        pair_proj.T,
        ada_scale_w,
        adaptive_shift_weight,
        pair_cond,
        qkvg_weight,
        out_gate_w,
        output_weight,
        transition_input_weight,
        trans_out,
    )
    return mixed.astype(BF16)


def solution(mesh):
    return jax.shard_map(
        functools.partial(shards, mesh.shape["row"], mesh.shape["col"]),
        mesh=mesh,
        in_specs=(
            P(None, "row", None),
            P("row", None),
            P("row", "col", None),
            P(),
            P(None, None, "col"),
            P(None, "col"),
            P(None, None, "col"),
            P(),
            P(),
            P(None, None, "col"),
            P("col"),
            P("col", None),
            P(None, None, "col"),
            P(None, "col"),
            P(None, None, "col"),
            P("col", None),
        ),
        out_specs=P(None, "row", "col"),
        check_vma=False,
    )
```

```python
import functools
import math

import jax
import jax.numpy as jnp
from jax import lax
from jax.experimental import pallas as pl
from jax.experimental.pallas import tpu as pltpu
from jax.sharding import PartitionSpec as P

H = 16
PARTS = 2
epsilon = 1e-05
F32 = jnp.float32
BF16 = jnp.bfloat16


def layer_norm(values):
    center = values - jnp.mean(values, axis=-1, keepdims=True)
    spread = jnp.mean(center * center, axis=-1, keepdims=True)
    return center * lax.rsqrt(spread + epsilon)


def dot(a, b):
    return jnp.dot(a, b, preferred_element_type=F32)


def dot_t(a, b):
    return lax.dot_general(a, b, (((1,), (1,)), ((), ())), preferred_element_type=F32)


class Exchange:
    def __init__(self, axis, n, source, buffer, send, recv):
        self.axis, self.n, self.source, self.buffer = axis, n, source, buffer
        self.send, self.recv = send, recv
        self.me = lax.axis_index(axis)

    def copy(self, d):
        target = lax.rem(self.me + d, self.n)
        return pltpu.make_async_remote_copy(
            src_ref=self.source(target),
            dst_ref=self.buffer.at[self.me],
            send_sem=self.send.at[d],
            recv_sem=self.recv.at[self.me],
            device_id={self.axis: target},
            device_id_type=pl.DeviceIdType.MESH,
        )

    def start(self):
        for d in range(1, self.n):
            self.copy(d).start()

    def arrive(self):
        for d in range(1, self.n):
            origin = lax.rem(self.me + d, self.n)
            pltpu.make_async_remote_copy(
                src_ref=self.buffer.at[origin],
                dst_ref=self.buffer.at[origin],
                send_sem=self.send.at[d],
                recv_sem=self.recv.at[origin],
                device_id={self.axis: origin},
                device_id_type=pl.DeviceIdType.MESH,
            ).wait_recv()

    def drain(self):
        for d in range(1, self.n):
            self.copy(d).wait_send()


class PairGather:
    def __init__(self, axis, n, buffer, send, handed, recv):
        self.axis, self.n, self.buffer = axis, n, buffer
        self.send, self.handed, self.recv = send, handed, recv
        self.me = lax.axis_index(axis)
        self.partner = self.me + 1 - 2 * lax.rem(self.me, 2)

    def copy(self, block, target, sem):
        return pltpu.make_async_remote_copy(
            src_ref=self.buffer.at[block],
            dst_ref=self.buffer.at[block],
            send_sem=sem,
            recv_sem=self.recv.at[block],
            device_id={self.axis: target},
            device_id_type=pl.DeviceIdType.MESH,
        )

    def mate(self, d):
        return lax.rem(self.me + 2 * d, self.n)

    def start(self):
        for d in range(1, self.n // 2):
            self.copy(self.me, self.mate(d), self.send.at[d]).start()
        self.copy(self.me, self.partner, self.send.at[0]).start()

    def hand_on(self):
        for d in range(1, self.n // 2):
            block = self.mate(d)
            self.copy(block, self.partner, self.handed.at[d]).wait_recv()
            self.copy(block, self.partner, self.handed.at[d]).start()

    def arrive(self):
        for d in range(self.n // 2):
            block = lax.rem(self.partner + 2 * d, self.n)
            self.copy(block, self.partner, self.send.at[0]).wait_recv()

    def drain(self):
        for d in range(1, self.n // 2):
            self.copy(self.me, self.mate(d), self.send.at[d]).wait_send()
            self.copy(self.mate(d), self.partner, self.handed.at[d]).wait_send()
        self.copy(self.me, self.partner, self.send.at[0]).wait_send()


class LineGather:
    def __init__(self, axis, n, buffer, send, handed, recv):
        self.axis, self.n, self.buffer = axis, n, buffer
        self.send, self.handed, self.recv = send, handed, recv
        self.me = lax.axis_index(axis)
        self.side = lax.rem(self.me, 2)
        self.place = self.me // 2
        self.length = n // 2
        self.partner = self.me + 1 - 2 * self.side

    def copy(self, block, target, sem):
        return pltpu.make_async_remote_copy(
            src_ref=self.buffer.at[block],
            dst_ref=self.buffer.at[block],
            send_sem=sem,
            recv_sem=self.recv.at[block],
            device_id={self.axis: target},
            device_id_type=pl.DeviceIdType.MESH,
        )

    def upward(self, k):
        return self.copy(self.me - 2 * k, self.me + 2, self.send.at[k])

    def downward(self, k):
        return self.copy(self.me + 2 * k, self.me - 2, self.send.at[self.length + k])

    def from_below(self, k):
        return self.copy(self.me - 2 * k, self.partner, self.handed.at[k])

    def from_above(self, k):
        return self.copy(self.me + 2 * k, self.partner, self.handed.at[self.length + k])

    def start(self):
        pl.when(self.place < self.length - 1)(lambda: self.upward(0).start())
        pl.when(self.place > 0)(lambda: self.downward(0).start())
        self.from_below(0).start()

    def step(self, k):
        @pl.when(self.place >= k)
        def _():
            self.from_below(k).wait_recv()
            pl.when(self.place < self.length - 1)(lambda: self.upward(k).start())
            self.from_below(k).start()

        @pl.when(self.place < self.length - k)
        def _():
            self.from_above(k).wait_recv()
            pl.when(self.place > 0)(lambda: self.downward(k).start())
            self.from_above(k).start()

    def arrive(self):
        for d in range(self.length):
            self.copy(2 * d + 1 - self.side, self.partner, self.send.at[0]).wait_recv()

    def drain(self):
        self.from_below(0).wait_send()
        for k in range(self.length):
            below = self.place >= k
            above = self.place < self.length - k
            last = self.place == self.length - 1
            first = self.place == 0
            pl.when(below & ~last)(lambda k=k: self.upward(k).wait_send())
            pl.when(above & ~first)(lambda k=k: self.downward(k).wait_send())
            if k:
                pl.when(below)(lambda k=k: self.from_below(k).wait_send())
                pl.when(above)(lambda k=k: self.from_above(k).wait_send())


def kernel(
    n_row,
    n_col,
    tokens_ref,
    single_ref,
    ada_gain_ref,
    scale_b_ref,
    query_b_ref,
    gate_b_ref,
    pair_gain_ref,
    pair_proj_ref,
    scale_w_hbm,
    shift_w_hbm,
    pair_hbm,
    qkvg_hbm,
    gate_w_hbm,
    out_w_hbm,
    trans_in_hbm,
    trans_out_hbm,
    out_ref,
    scale_w,
    shift_w,
    pair,
    qkvg,
    gate_w,
    trans_in,
    trans_out,
    out_w,
    mods0,
    mods1,
    bias_tx,
    bias_rx,
    kv,
    attended,
    terms32,
    terms_tx,
    terms_rx,
    resid_parts,
    load_sem,
    mods0_send,
    mods0_recv,
    mods1_send,
    mods1_recv,
    bias_send,
    bias_recv,
    att_send,
    att_recv,
    terms_send,
    terms_recv,
    w_send,
    w_hand,
    w_recv,
    kv_send,
    kv_hand,
    kv_recv,
):
    row, col = lax.axis_index("row"), lax.axis_index("col")
    samples, rows, full = tokens_ref.shape
    width = qkvg.shape[1]
    size = full // H
    heads = width // size
    flat = samples * rows
    some = samples // PARTS
    part_flat = flat // PARTS

    loads = {}
    for number, (name, source, target) in enumerate(
        (
            ("scale", scale_w_hbm, scale_w),
            ("shift", shift_w_hbm, shift_w),
            ("pair", pair_hbm, pair),
            ("gate", gate_w_hbm, gate_w),
            ("qkvg", qkvg_hbm, qkvg),
            ("out", out_w_hbm, out_w.at[col]),
            ("in", trans_in_hbm, trans_in),
            ("back", trans_out_hbm, trans_out),
        )
    ):
        loads[name] = pltpu.make_async_copy(source, target, load_sem.at[number])
        loads[name].start()

    mods0_x = Exchange("col", n_col, lambda t: mods0.at[col], mods0, mods0_send, mods0_recv)
    mods1_x = Exchange("col", n_col, lambda t: mods1.at[col], mods1, mods1_send, mods1_recv)
    bias_x = Exchange(
        "col", n_col, lambda t: bias_tx.at[pl.ds(t * heads, heads)], bias_rx, bias_send, bias_recv
    )
    att_x = Exchange("col", n_col, lambda t: attended.at[col], attended, att_send, att_recv)
    terms_x = Exchange("col", n_col, lambda t: terms_tx.at[t], terms_rx, terms_send, terms_recv)
    w_x = PairGather("col", n_col, out_w, w_send, w_hand, w_recv)
    kv_x = [
        LineGather("row", n_row, kv.at[g], kv_send.at[g], kv_hand.at[g], kv_recv.at[g])
        for g in range(PARTS)
    ]

    barrier = pltpu.get_barrier_semaphore()
    for d in range(1, n_col):
        pl.semaphore_signal(
            barrier,
            inc=1,
            device_id={"col": lax.rem(col + d, n_col)},
            device_id_type=pl.DeviceIdType.MESH,
        )
    for target in [lax.rem(row + 2 * d, n_row) for d in range(1, n_row // 2)] + [kv_x[0].partner]:
        pl.semaphore_signal(
            barrier, inc=1, device_id={"row": target}, device_id_type=pl.DeviceIdType.MESH
        )

    base = layer_norm(single_ref[...].astype(F32))
    cond0 = (base * ada_gain_ref[0:1, :]).astype(BF16)
    cond1 = (base * ada_gain_ref[1:2, :]).astype(BF16)
    loads["scale"].wait()
    loads["shift"].wait()
    scale0 = jax.nn.sigmoid(dot_t(cond0, scale_w[0]) + scale_b_ref[0:1, :])
    shift0 = dot_t(cond0, shift_w[0])
    mods0[col] = jnp.concatenate([scale0, shift0], axis=0).astype(BF16)
    pl.semaphore_wait(barrier, n_col - 1 + n_row // 2)
    mods0_x.start()

    loads["pair"].wait()
    proj = pair_proj_ref[...]
    proj_hi = proj.astype(BF16)
    proj_lo = (proj - proj_hi.astype(F32)).astype(BF16)
    proj_both = jnp.concatenate(
        [
            jnp.concatenate([proj_hi, proj_hi], axis=1),
            jnp.concatenate([proj_lo, proj_lo], axis=1),
        ],
        axis=0,
    )
    gain = pair_gain_ref[...]

    def bias_step(step, carry):
        first = pl.multiple_of(step * 8, 8)
        found = []
        for k in range(8):
            normed = layer_norm(pair[first + k]) * gain
            high = normed.astype(BF16)
            low = (normed - high.astype(F32)).astype(BF16)
            both = dot_t(proj_both, jnp.concatenate([high, low], axis=1))
            found.append(both[:H] + both[H:])
        stacked = jnp.stack(found, axis=0)
        bias_tx[:, pl.ds(first, 8), :] = jnp.transpose(stacked, (1, 0, 2))
        return carry

    lax.fori_loop(0, rows // 8, bias_step, 0)
    bias_x.start()

    tokens = tokens_ref[...].astype(F32)
    tokens_normed = layer_norm(tokens)

    def across(parts, first):
        return jnp.concatenate([p[first * rows : (first + 1) * rows] for p in parts], axis=1)

    mods0_x.arrive()
    parts = [mods0[c].astype(F32) for c in range(n_col)]
    norm_in = across(parts, 0)[None] * tokens_normed + across(parts, 1)[None]
    norm_in = norm_in.reshape(flat, full).astype(BF16)
    loads["qkvg"].wait()
    key = dot_t(norm_in, qkvg[1])
    value = dot_t(norm_in, qkvg[2])
    for g in range(PARTS):
        span = slice(g * part_flat, (g + 1) * part_flat)
        kv[g, row] = jnp.concatenate([key[span], value[span]], axis=1).astype(BF16)
    first, second = kv_x
    steps = n_row // 2
    first.start()
    second.start()

    loads["gate"].wait()
    gate0 = jax.nn.sigmoid(dot_t(cond0, gate_w[0]) + gate_b_ref[0:1, :])
    scale1 = jax.nn.sigmoid(dot_t(cond1, scale_w[1]) + scale_b_ref[1:2, :])
    shift1 = dot_t(cond1, shift_w[1])
    fill = jnp.zeros((mods1.shape[1] - 3 * rows, width), F32)
    mods1[col] = jnp.concatenate([gate0, scale1, shift1, fill], axis=0).astype(BF16)
    mods1_x.start()
    loads["out"].wait()
    w_x.start()
    first.step(1)
    second.step(1)

    query = (dot_t(norm_in, qkvg[0]) + query_b_ref[...]).astype(BF16).astype(F32)
    gates = jax.nn.sigmoid(dot_t(norm_in, qkvg[3]))
    gate1 = jax.nn.sigmoid(dot_t(cond1, gate_w[1]) + gate_b_ref[1:2, :])
    lane = lax.broadcasted_iota(jnp.int32, (rows, width), 1)
    masks = [(lane >= h * size) & (lane < (h + 1) * size) for h in range(heads)]
    bias_rx[col] = bias_tx[pl.ds(col * heads, heads)]
    bias_x.arrive()
    per_block = n_row // n_col

    half = flat // 2

    def pack(array):
        return jnp.concatenate([array[:half], array[half:]], axis=1)

    def unpack(array):
        return jnp.concatenate([array[:, :width], array[:, width:]], axis=0)

    def tokens_of(g, which, b, s):
        lanes = slice(which * width, (which + 1) * width)
        return jnp.concatenate(
            [
                kv[g, b * per_block + r].astype(F32)[s * rows : (s + 1) * rows, lanes]
                for r in range(per_block)
            ],
            axis=0,
        ).astype(BF16)

    def attend(g):
        results = []
        for s in range(some):
            span = slice((g * some + s) * rows, (g * some + s + 1) * rows)
            stacked_query = jnp.concatenate(
                [jnp.where(mask, query[span], 0.0) for mask in masks], axis=0
            ).astype(BF16)
            scores = []
            for b in range(n_col):
                bias = bias_rx[b].reshape(heads * rows, per_block * rows)
                score = dot_t(stacked_query, tokens_of(g, 0, b, s))
                scores.append(score * (1.0 / math.sqrt(size)) + bias)
            peak = functools.reduce(jnp.maximum, scores)
            peak = jnp.max(peak, axis=-1, keepdims=True)
            scores = [jnp.exp(score - peak) for score in scores]
            total = jnp.sum(functools.reduce(jnp.add, scores), axis=-1, keepdims=True)
            accum = jnp.zeros((heads * rows, width), F32)
            for b in range(n_col):
                accum = accum + dot(scores[b].astype(BF16), tokens_of(g, 1, b, s))
            accum = accum / total
            mine = jnp.zeros((rows, width), F32)
            for h in range(heads):
                mine = jnp.where(masks[h], accum[h * rows : (h + 1) * rows], mine)
            results.append(gates[span] * mine)
        return results

    for k in range(2, steps):
        first.step(k)
        second.step(k)
    w_x.hand_on()
    first.arrive()
    results = attend(0)
    second.arrive()
    results = results + attend(1)
    attended[col] = pack(jnp.concatenate(results, axis=0)).astype(BF16)
    att_x.start()
    mods1_x.arrive()
    parts = [mods1[c].astype(F32) for c in range(n_col)]
    gate0_all, scale1_all, shift1_all = (across(parts, k)[None] for k in range(3))
    w_x.arrive()
    loads["in"].wait()
    loads["back"].wait()
    att_x.arrive()
    projected = jnp.zeros((flat, full), F32)
    for c in range(n_col):
        projected = projected + dot(unpack(attended[c].astype(F32)).astype(BF16), out_w[c])
    resid = tokens + gate0_all * projected.reshape(samples, rows, full)
    middle = (scale1_all * layer_norm(resid) + shift1_all).reshape(flat, full).astype(BF16)
    inner = dot(middle, trans_in[0])
    hidden = (jax.nn.silu(inner) * dot(middle, trans_in[1])).astype(BF16)
    terms = dot(hidden, trans_out[...])
    for c in range(n_col):
        part = pack(terms[:, c * width : (c + 1) * width])
        terms32[c] = part
        terms_tx[c] = part.astype(BF16)
    terms_x.start()
    resid = resid.reshape(flat, full)
    for c in range(n_col):
        resid_parts[c] = resid[:, c * width : (c + 1) * width]
    outward = terms32[col]
    terms_x.arrive()
    for d in range(1, n_col):
        outward = outward + terms_rx[lax.rem(col + d, n_col)].astype(F32)
    outward = unpack(outward).reshape(samples, rows, width)
    mixed = resid_parts[col].reshape(samples, rows, width) + gate1[None] * outward
    out_ref[...] = mixed

    for exchange in [mods0_x, bias_x, mods1_x, w_x, att_x, terms_x] + kv_x:
        exchange.drain()


def shards(
    n_row,
    n_col,
    tokens,
    single_cond,
    pair_cond,
    ada_gain,
    ada_scale_w,
    ada_scale_b,
    adaptive_shift_weight,
    pair_gain,
    pair_proj,
    qkvg_weight,
    query_bias,
    output_weight,
    out_gate_w,
    out_gate_b,
    transition_input_weight,
    trans_out,
):
    samples, rows, full = tokens.shape
    width = qkvg_weight.shape[2]
    heads = width * H // full
    flat = samples * rows
    keys_here = pair_cond.shape[1]
    ada_scale_w, adaptive_shift_weight, qkvg_weight, out_gate_w = (
        jnp.swapaxes(array, 1, 2)
        for array in (ada_scale_w, adaptive_shift_weight, qkvg_weight, out_gate_w)
    )
    vmem = pl.BlockSpec(memory_space=pltpu.VMEM)
    hbm = pl.BlockSpec(memory_space=pl.ANY)

    def like(array):
        return pltpu.VMEM(array.shape, array.dtype)

    def sems(*shape):
        return pltpu.SemaphoreType.DMA(shape)

    mixed = pl.pallas_call(
        functools.partial(kernel, n_row, n_col),
        out_shape=jax.ShapeDtypeStruct((samples, rows, width), F32),
        in_specs=[vmem] * 8 + [hbm] * 8,
        out_specs=vmem,
        scratch_shapes=[
            like(ada_scale_w),
            like(adaptive_shift_weight),
            like(pair_cond),
            like(qkvg_weight),
            like(out_gate_w),
            like(transition_input_weight),
            like(trans_out),
            pltpu.VMEM((n_col,) + output_weight.shape, BF16),
            pltpu.VMEM((n_col, 2 * rows, width), BF16),
            pltpu.VMEM((n_col, -(-3 * rows // 16) * 16, width), BF16),
            pltpu.VMEM((H, rows, keys_here), F32),
            pltpu.VMEM((n_col, heads, rows, keys_here), F32),
            pltpu.VMEM((PARTS, n_row, flat // PARTS, 2 * width), BF16),
            pltpu.VMEM((n_col, flat // 2, 2 * width), BF16),
            pltpu.VMEM((n_col, flat // 2, 2 * width), F32),
            pltpu.VMEM((n_col, flat // 2, 2 * width), BF16),
            pltpu.VMEM((n_col, flat // 2, 2 * width), BF16),
            pltpu.VMEM((n_col, flat, width), F32),
            sems(8),
        ]
        + [sems(n_col)] * 13
        + [sems(PARTS, n_row)] * 3,
        compiler_params=pltpu.CompilerParams(
            collective_id=0, has_side_effects=True, vmem_limit_bytes=56 * 1024 * 1024
        ),
    )(
        tokens,
        single_cond,
        ada_gain,
        ada_scale_b,
        query_bias[None],
        out_gate_b,
        pair_gain[None],
        pair_proj.T,
        ada_scale_w,
        adaptive_shift_weight,
        pair_cond,
        qkvg_weight,
        out_gate_w,
        output_weight,
        transition_input_weight,
        trans_out,
    )
    return mixed.astype(BF16)


def solution(mesh):
    return jax.shard_map(
        functools.partial(shards, mesh.shape["row"], mesh.shape["col"]),
        mesh=mesh,
        in_specs=(
            P(None, "row", None),
            P("row", None),
            P("row", "col", None),
            P(),
            P(None, None, "col"),
            P(None, "col"),
            P(None, None, "col"),
            P(),
            P(),
            P(None, None, "col"),
            P("col"),
            P("col", None),
            P(None, None, "col"),
            P(None, "col"),
            P(None, None, "col"),
            P("col", None),
        ),
        out_specs=P(None, "row", "col"),
        check_vma=False,
    )
```
